512 devices in a mesh: section: 32 (over y, x), tp: 16 (over z, core).
Axes of the slice: x: 4, y: 8, z: 8, core: 2. Of those that a mesh axis runs over, the one named last changes fastest.
Arguments:
- leave_query: bfloat16 [32, 256, 4096], P('section', None, 'tp'), may hold values from -150 to 150
- leave_key: bfloat16 [32, 256, 4096], P('section', None, 'tp'), may hold values from -6 to 6
- leave_value: bfloat16 [32, 256, 4096], P('section', None, 'tp'), may hold values from -6 to 6
- arrive_query: bfloat16 [32, 256, 4096], P('section', None, 'tp'), may hold values from -150 to 150
- arrive_key: bfloat16 [32, 256, 4096], P('section', None, 'tp'), may hold values from -6 to 6
- arrive_value: bfloat16 [32, 256, 4096], P('section', None, 'tp'), may hold values from -6 to 6
- leave_residual: bfloat16 [32, 256, 6144], P('section', 'tp'), may hold values from -6 to 6
- out_weight: bfloat16 [32, 4096, 6144], P('section', 'tp'), may hold values from -0.5 to 0.5
- gate_scale: float32 [32, 6144], P('section'), may hold values from 0.25 to 1.75
- sign_bits: int32 [6144], replicated, may hold values 0 or 1
Outputs:
- arrived: bfloat16 [32, 256, 6144], P('section', 'tp')
The draws below stay inside these ranges and needn't reach their ends.
All inputs are finite; a program needn't handle non-finite values.
Results may differ from the reference program's by a relative error of at most 0.0063.
Values may be sent and summed in bfloat16 or wider, within the bound.
A program may use at most 64 MiB of HBM per device.

```python
import math
import jax
import jax.numpy as jnp
from jax import lax

D = 6144
HD = 128
HEADS_DEV = 2
BLK = 128
TOK = 256
HEADS = 32
SECTIONS = 32
N_TP = 16


def common_normals(key, salt):
    drawn = jax.random.normal(jax.random.fold_in(key, salt), (SECTIONS, TOK, HEADS * HD), jnp.float32)
    return jnp.clip(drawn, -6.0, 6.0)


def keys_drawn(key, salt):
    shared = common_normals(key, salt)
    return shared.astype(jnp.bfloat16)


def queries_drawn(key, own_key):
    own = 1.5 * jnp.clip(jax.random.normal(own_key, (SECTIONS, TOK, HEADS * HD), jnp.float32), -4.0, 4.0)
    return own.astype(jnp.bfloat16)


def draw_leave_key(key, part):
    return keys_drawn(key, 101)


def draw_arrive_key(key, part):
    return keys_drawn(key, 102)


def draw_leave_query(key, part):
    own_key = jax.random.fold_in(key, 3)
    return queries_drawn(key, own_key)


def draw_arrive_query(key, part):
    own_key = jax.random.fold_in(key, 4)
    return queries_drawn(key, own_key)


def set_ends(values, rng, least, high):
    longest = values.shape.index(max(values.shape))
    spots = []
    for shift in (0, 1):
        where = [jax.random.randint(jax.random.fold_in(rng, axis), (), 0, length) for axis, length in enumerate(values.shape)]
        where[longest] = (where[longest] + shift) % values.shape[longest]
        spots.append(tuple(where))
    return values.at[spots[0]].set(least).at[spots[1]].set(high)


def block_levels(stream_key, extent, split, least, top_value):
    def one(dim, shards_of):
        draws = jax.random.uniform(jax.random.fold_in(jax.random.fold_in(stream_key, 6), dim), (shards_of,), jnp.float32, least / len(split), top_value / len(split))
        return jnp.repeat(jnp.exp(draws), extent[dim] // shards_of).reshape((-1,) + (1,) * (len(extent) - dim - 1))

    level = one(*split[0])
    for cut in split[1:]:
        level = level * one(*cut)
    return level


def gaussian(rng, extent, scale, most, split=(), held_as=jnp.bfloat16):
    values = jax.random.normal(rng, extent, jnp.float32) * scale
    if len(split) > 0:
        values = block_levels(rng, extent, split, -0.22, 0.18) * values
    return jnp.clip(values, min=-most, max=most).astype(held_as)


def setup_inputs(seed: int = 0) -> dict:
    splits = jax.random.split(jax.random.key(seed), 11)
    leave_query = draw_leave_query(jax.random.fold_in(splits[10], 71), 0)
    leave_key = draw_leave_key(jax.random.fold_in(splits[10], 71), 0)
    leave_value = gaussian(splits[2], (SECTIONS, TOK, HEADS * HD), 1.0, 6.0, ((0, 32), (2, 16)))
    arrive_query = draw_arrive_query(jax.random.fold_in(splits[10], 71), 0)
    arrive_key = draw_arrive_key(jax.random.fold_in(splits[10], 71), 0)
    arrive_value = gaussian(splits[5], (SECTIONS, TOK, HEADS * HD), 1.0, 6.0, ((0, 32), (2, 16)))
    leave_residual = gaussian(splits[6], (SECTIONS, TOK, D), 1.0, 6.0, ((0, 32), (1, 16)))
    out_weight = gaussian(splits[7], (SECTIONS, HEADS * HD, D), HD ** -0.5, 0.5, ((0, 32), (1, 16)))
    gate_scale = jnp.clip(0.25 + 1.5 * jax.random.uniform(splits[8], (SECTIONS, D), jnp.float32) ** block_levels(splits[8], (SECTIONS, D), ((0, 32),), -0.2, 0.2), 0.25, 1.75)
    sign_bits = set_ends((jax.random.randint(splits[9], (D,), 0, 2) < 1).astype(jnp.int32), jax.random.fold_in(splits[9], 1), 0, 1)
    return {"leave_query": leave_query, "leave_key": leave_key, "leave_value": leave_value, "arrive_query": arrive_query, "arrive_key": arrive_key, "arrive_value": arrive_value, "leave_residual": leave_residual, "out_weight": out_weight, "gate_scale": gate_scale, "sign_bits": sign_bits}


def hadamard_matrix(order):
    index = jnp.arange(order, dtype=jnp.int32)
    anded = jnp.bitwise_and(index[:, None], index[None, :])
    parity = jnp.zeros((order, order), jnp.int32)
    for bit_number in range(order.bit_length() - 1):
        parity = parity + jnp.bitwise_and(jnp.right_shift(anded, bit_number), 1)
    signed = 1.0 - 2.0 * jnp.bitwise_and(parity, 1).astype(jnp.float32)
    return signed / math.sqrt(order)

def attend(query_rows, key_rows, value_rows):
    count = query_rows.shape[0]
    query_heads = query_rows.reshape(count, -1, HD).astype(jnp.float32)
    key_heads = key_rows.reshape(count, -1, HD).astype(jnp.float32)
    value_heads = value_rows.reshape(count, -1, HD).astype(jnp.float32)
    scores = jnp.einsum('qhd,khd->hqk', query_heads, key_heads) / math.sqrt(HD)
    peak = lax.optimization_barrier(jnp.max(scores, axis=-1, keepdims=True))
    raised = jnp.exp(scores - peak)
    probs = (raised / lax.optimization_barrier(jnp.sum(raised, axis=-1, keepdims=True))).astype(jnp.bfloat16)
    mixed = jnp.einsum('hqk,khd->qhd', probs.astype(jnp.float32), value_heads)
    return mixed.astype(jnp.bfloat16).reshape(count, -1)

def rotate(summed, hadamard_table, sign_row):
    row_count = summed.shape[0]
    blocks = summed.reshape(row_count, -1, BLK) * sign_row.reshape(-1, BLK)
    rotated = jnp.einsum('rnb,bc->rnc', blocks, hadamard_table, precision=lax.Precision.HIGHEST)
    return rotated.reshape(row_count, -1)

def group_sum(query_rows, key_rows, value_rows, weight_rows, gate_row):
    width = HEADS_DEV * HD

    def add_group(totals, group):
        start = (group * width).astype(jnp.int32)
        attended = attend(lax.dynamic_slice_in_dim(query_rows, start, width, 1), lax.dynamic_slice_in_dim(key_rows, start, width, 1), lax.dynamic_slice_in_dim(value_rows, start, width, 1))
        weights = lax.dynamic_slice_in_dim(weight_rows, start, width, 0)
        partial_value = (jnp.dot(attended, weights, preferred_element_type=jnp.float32) * gate_row).astype(jnp.bfloat16)
        partial_value = lax.optimization_barrier(partial_value)
        return (totals + partial_value.astype(jnp.float32), None)
    totals, _ = lax.scan(add_group, jnp.zeros((TOK, D), jnp.float32), jnp.arange(N_TP, dtype=jnp.int32))
    return totals

def reference(leave_query, leave_key, leave_value, arrive_query, arrive_key, arrive_value, leave_residual, out_weight, gate_scale, sign_bits):
    hadamard_table = hadamard_matrix(BLK)
    sign_row = 1.0 - 2.0 * sign_bits.astype(jnp.float32)

    def one_section(pieces):
        l_query, l_key, l_value, a_query, a_key, a_value, residual, weight_rows, gate_row = pieces
        leave_total = rotate(group_sum(l_query, l_key, l_value, weight_rows, gate_row), hadamard_table, sign_row)
        arrive_total = rotate(group_sum(a_query, a_key, a_value, weight_rows, gate_row), hadamard_table, sign_row)
        handed = (residual.astype(jnp.float32) + leave_total).astype(jnp.bfloat16)
        return (handed, arrive_total)
    handed, arrive_totals = lax.map(one_section, (leave_query, leave_key, leave_value, arrive_query, arrive_key, arrive_value, leave_residual, out_weight, gate_scale))
    passed = jnp.roll(handed, 1, axis=0)
    return (passed.astype(jnp.float32) + arrive_totals).astype(jnp.bfloat16)
```

```python
import functools
import math

import jax
import jax.numpy as jnp
from jax import lax
from jax.experimental import pallas as pl
from jax.experimental.pallas import tpu as pltpu
from jax.sharding import PartitionSpec as P

HD = 128
BLK = 128
WIDE = 512
CHAINS = ((1, 4, 2), (-1, 3, 1))
MESH = pl.DeviceIdType.MESH
F32 = jnp.float32
BF16 = jnp.bfloat16


def kernel(
    lq, lk, lv, aq, ak, av, residual, weight, gate, sign_bits,
    out,
    qkv, qkv_sem,
    wbuf, w_sem, w_send, w_recv,
    att, att_send, att_recv,
    resbuf, res_sem, res_send, res_recv,
    table, signs, gates, gate_sem, sign_sem, bits_v,
    sums,
    zs, zr, zs_sem, zr_sem,
    xs, xr, xs_sem, xr_sem,
    fin, fs_sem, fin_sem,
    own0, own_keep, own_s, own_r, os_sem, or_sem,
    staged, out_sem,
):
    sections = lax.axis_size("section")
    chips = lax.axis_size("tp") // 2
    s = lax.axis_index("section")
    tp = lax.axis_index("tp")
    z = tp // 2
    c = tp % 2
    other = 1 - c
    tokens = lq.shape[1]
    kd = lq.shape[2]
    width = residual.shape[2]
    half = width // 2
    pieces = half // WIDE
    rows = tokens // chips
    mine = rows // 2

    next_section = {"section": lax.rem(s + 1, sections)}
    prev_section = {"section": lax.rem(s + sections - 1, sections)}
    partner = {"tp": 2 * z + other}

    def chip(at):
        return lax.rem(at + 2 * chips, chips)

    def turn(p, sign):
        return sign * (1 - 2 * lax.rem(p + c, 2))

    def cols(p, which):
        return pl.ds(pl.multiple_of(which * half + p * WIDE, 128), WIDE)

    loads = []
    for i, ref in enumerate((lq, lk, lv, aq, ak, av)):
        loads.append(pltpu.make_async_copy(ref.at[0], qkv.at[i], qkv_sem.at[i]))
        loads[-1].start()
    gate_copy = pltpu.make_async_copy(gate, gates, gate_sem)
    gate_copy.start()
    sign_copy = pltpu.make_async_copy(sign_bits, bits_v, sign_sem)
    sign_copy.start()

    def w_local(p):
        return pltpu.make_async_copy(weight.at[0, :, cols(p, c)], wbuf.at[p, pl.ds(0, kd)], w_sem.at[p])

    def w_remote(p):
        return pltpu.make_async_remote_copy(
            weight.at[0, :, cols(p, other)], wbuf.at[p, pl.ds(kd, kd)], w_send.at[p], w_recv.at[p],
            device_id=partner, device_id_type=MESH)

    def loop(body):
        lax.fori_loop(0, pieces, lambda p, _: (body(p), None)[1], None)

    loop(lambda p: w_local(p).start())
    own_rows = pl.ds(pl.multiple_of(mine * c, mine), mine)
    other_rows = pl.ds(pl.multiple_of(mine * other, mine), mine)
    res_local = pltpu.make_async_copy(
        residual.at[0, :, pl.ds(pl.multiple_of(c * half, 128), half)], resbuf.at[own_rows], res_sem)
    res_local.start()

    barrier = pltpu.get_barrier_semaphore()
    greeted = [partner, next_section, prev_section]
    for step in (1, -1):
        for core in (0, 1):
            greeted.append({"tp": 2 * chip(z + step) + core})
    for device in greeted:
        pl.semaphore_signal(barrier, inc=1, device_id=device, device_id_type=MESH)
    pl.semaphore_wait(barrier, len(greeted))

    loop(lambda p: w_remote(p).start())
    res_remote = pltpu.make_async_remote_copy(
        residual.at[0, :, pl.ds(pl.multiple_of(other * half, 128), half)], resbuf.at[own_rows], res_send, res_recv,
        device_id=partner, device_id_type=MESH)
    res_remote.start()

    def att_copy(m):
        there = att.at[pl.ds(m * tokens, tokens), pl.ds(kd, kd)]
        here = att.at[pl.ds(m * tokens, tokens), pl.ds(0, kd)]
        return pltpu.make_async_remote_copy(
            here, there, att_send.at[m], att_recv.at[m], device_id=partner, device_id_type=MESH)

    for m in range(2):
        for i in range(3):
            loads[3 * m + i].wait()
        for h in range(kd // HD):
            lanes = pl.ds(h * HD, HD)
            query, key, value = (qkv[3 * m + i, :, lanes] for i in range(3))
            scores = lax.dot_general(query, key, (((1,), (1,)), ((), ())), preferred_element_type=F32)
            scores = scores * (1.0 / math.sqrt(HD))
            peak = jnp.max(scores, axis=-1, keepdims=True)
            raised = jnp.exp(scores - peak)
            probs = (raised / jnp.sum(raised, axis=-1, keepdims=True)).astype(BF16)
            mixed = jnp.dot(probs, value, preferred_element_type=F32)
            att[pl.ds(m * tokens, tokens), lanes] = mixed.astype(BF16)
        att_copy(m).start()

    i = lax.broadcasted_iota(jnp.int32, (BLK, BLK), 0)
    j = lax.broadcasted_iota(jnp.int32, (BLK, BLK), 1)
    anded = i & j
    anded = anded ^ (anded >> 4)
    anded = anded ^ (anded >> 2)
    anded = anded ^ (anded >> 1)
    table[...] = (1 - 2 * (anded & 1)).astype(F32).astype(BF16)
    sign_copy.wait()
    signs[...] = 1.0 - 2.0 * bits_v[...].astype(F32)

    def turned(values):
        r = values.shape[0]
        blocks = jnp.concatenate([values[:, b * BLK:(b + 1) * BLK] for b in range(WIDE // BLK)], axis=0)
        made = jnp.dot(blocks, table[...], preferred_element_type=F32)
        return jnp.concatenate([made[b * r:(b + 1) * r] for b in range(WIDE // BLK)], axis=1)

    gate_copy.wait()
    res_local.wait()
    res_remote.wait_recv()
    for m in range(2):
        att_copy(m).wait_recv()

    def leaving(p, at):
        return sums[p, pl.ds(pl.multiple_of(rows * at, rows), rows), :]

    def arriving(p, at):
        return sums[p, pl.ds(pl.multiple_of(tokens + rows * at, rows), rows), :]

    def z_copy(ch, j, p):
        sign, _, _ = CHAINS[ch]
        to = {"tp": 2 * chip(z + turn(p, sign)) + c}
        return pltpu.make_async_remote_copy(
            zs[ch][j].at[p], zr[ch][j].at[p], zs_sem.at[ch, j, p], zr_sem.at[ch, j, p], device_id=to, device_id_type=MESH)

    def fin_copy(ch, core, p):
        sign, _, _ = CHAINS[ch]
        to = {"tp": 2 * chip(z + turn(p, sign)) + core}
        return pltpu.make_async_remote_copy(
            zs[ch][1].at[p, pl.ds(core * mine, mine)], fin.at[ch, c, p],
            fs_sem.at[ch, core, p], fin_sem.at[ch, c, p], device_id=to, device_id_type=MESH)

    def fin_arrival(ch, core, p):
        return pltpu.make_async_remote_copy(
            zs[ch][1].at[p, pl.ds(core * mine, mine)], fin.at[ch, core, p],
            fs_sem.at[ch, core, p], fin_sem.at[ch, core, p], device_id=partner, device_id_type=MESH)

    def x_copy(slot, p):
        return pltpu.make_async_remote_copy(
            xs.at[slot, p], xr.at[slot, p], xs_sem.at[slot, p], xr_sem.at[slot, p],
            device_id=next_section, device_id_type=MESH)

    def own_copy(p):
        return pltpu.make_async_remote_copy(
            own_s.at[p], own_r.at[p], os_sem.at[p], or_sem.at[p], device_id=partner, device_id_type=MESH)

    slots = {}
    for ch, (_, first, join) in enumerate(CHAINS):
        for j in range(1, join + 1):
            slots[ch, j] = len(slots) + 1

    def at(ch, j, p):
        return chip(z + j * turn(p, CHAINS[ch][0]))

    def apart(ch, j, p):
        first = CHAINS[ch][1]
        lead, tail = leaving(p, at(ch, j, p)), arriving(p, at(ch, j, p))
        if j < first:
            z_copy(ch, j + 1, p).wait_recv()
            lead = lead + zr[ch][j + 1][p, :rows].astype(F32)
            tail = tail + zr[ch][j + 1][p, rows:].astype(F32)
        zs[ch][j][p, :rows] = lead.astype(BF16)
        zs[ch][j][p, rows:] = tail.astype(BF16)
        z_copy(ch, j, p).start()

    def cross(ch, j, p):
        _, first, join = CHAINS[ch]
        lead = leaving(p, at(ch, j, p))
        if j == join and j < first:
            z_copy(ch, j + 1, p).wait_recv()
            lead = lead + zr[ch][j + 1][p, :rows].astype(F32)
        xs[slots[ch, j], p] = lead.astype(BF16)
        x_copy(slots[ch, j], p).start()

    def joined(ch, j, p):
        _, first, join = CHAINS[ch]
        x_copy(slots[ch, j], p).wait_recv()
        tail = arriving(p, at(ch, j, p)) + xr[slots[ch, j], p].astype(F32)
        if j < join:
            z_copy(ch, j + 1, p).wait_recv()
            tail = tail + zr[ch][j + 1][p].astype(F32)
        elif j < first:
            tail = tail + zr[ch][j + 1][p, rows:].astype(F32)
        zs[ch][j][p] = tail.astype(BF16)
        if j > 1:
            z_copy(ch, j, p).start()
        else:
            for core in (0, 1):
                fin_copy(ch, core, p).start()

    def own_cross(p):
        plain = turned(resbuf[:, pl.ds(pl.multiple_of(p * WIDE, 128), WIDE)])
        plain = plain * (signs[:, cols(p, c)] * (1.0 / math.sqrt(BLK)))
        xs[0, p] = (leaving(p, z) + plain).astype(BF16)
        x_copy(0, p).start()

    def own_joined(p):
        x_copy(0, p).wait_recv()
        own0[...] = arriving(p, z) + xr[0, p].astype(F32)
        own_keep[p] = own0[own_rows, :]
        own_s[p] = own0[other_rows, :].astype(BF16)
        own_copy(p).start()

    def project(p):
        w_local(p).wait()
        w_remote(p).wait_recv()
        made = jnp.dot(att[...], wbuf[p], preferred_element_type=F32)
        sums[p] = made * gates[:, cols(p, c)]

    def finish(core, p, own):
        for ch in range(len(CHAINS)):
            fin_arrival(ch, core, p).wait_recv()
        total = own + fin[0, core, p].astype(F32) + fin[1, core, p].astype(F32)
        total = total * signs[:, cols(p, core)]
        high = total.astype(BF16)
        low = (total - high.astype(F32)).astype(BF16)
        r = turned(jnp.concatenate([high, low], axis=0))
        r = (r[:mine] + r[mine:]) * (1.0 / math.sqrt(BLK))
        staged[core, p] = r.astype(BF16)
        out_copy(core, p).start()

    def out_copy(core, p):
        return pltpu.make_async_copy(staged.at[core, p], out.at[0, :, cols(p, core)], out_sem.at[core, p])

    def begin(p):
        project(p)
        for ch, (_, first, join) in enumerate(CHAINS):
            if first > join:
                apart(ch, first, p)
        own_cross(p)
        for ch, (_, first, join) in enumerate(CHAINS):
            for j in range(1, join + 1):
                if j < join or join == first:
                    cross(ch, j, p)

    loop(begin)
    most = max(first for _, first, _ in CHAINS)
    for back in range(1, most + 1):
        def middle(p, back=back):
            for ch, (_, first, join) in enumerate(CHAINS):
                j = first - back
                if j > join:
                    apart(ch, j, p)
                elif j == join:
                    cross(ch, j, p)

        def after(p, back=back):
            for ch, (_, first, join) in enumerate(CHAINS):
                j = first - back + 1
                if 1 <= j <= join:
                    joined(ch, j, p)

        loop(after)
        if any(first - back >= join for _, first, join in CHAINS):
            loop(middle)
        if back == most - 1:
            loop(own_joined)

    def finish_near(p):
        finish(c, p, own_keep[p])

    def finish_far(p):
        own_copy(p).wait_recv()
        finish(other, p, own_r[p].astype(F32))

    def finish_both(p):
        finish_near(p)
        finish_far(p)

    loop(finish_both)

    res_remote.wait_send()
    for m in range(2):
        att_copy(m).wait_send()

    def drain(p):
        w_remote(p).wait_send()
        for ch, (_, first, join) in enumerate(CHAINS):
            for j in range(2, first + 1):
                z_copy(ch, j, p).wait_send()
            for core in (0, 1):
                fin_copy(ch, core, p).wait_send()
        for slot in range(len(slots) + 1):
            x_copy(slot, p).wait_send()
        own_copy(p).wait_send()
        for core in (0, 1):
            out_copy(core, p).wait()

    loop(drain)


def local(
    leave_query, leave_key, leave_value, arrive_query, arrive_key, arrive_value,
    leave_residual, out_weight, gate_scale, sign_bits,
):
    tokens, kd = leave_query.shape[1:]
    width = leave_residual.shape[2]
    chips = lax.axis_size("tp") // 2
    rows, mine = tokens // chips, tokens // chips // 2
    half = width // 2
    pieces = half // WIDE
    dma = pltpu.SemaphoreType.DMA

    def hop_buffers():
        return [
            [None if j < 1 else pltpu.VMEM((pieces, 2 * rows if j > join else rows, WIDE), BF16)
             for j in range(first + 1)]
            for _, first, join in CHAINS
        ]

    def strip(tree):
        return [[pltpu.VMEM((1, 16, 128), BF16) if leaf is None else leaf for leaf in row] for row in tree]

    most = max(first for _, first, _ in CHAINS) + 1
    nx = 1 + sum(join for _, _, join in CHAINS)
    scratch = [
        pltpu.VMEM((6, tokens, kd), BF16), dma((6,)),
        pltpu.VMEM((pieces, 2 * kd, WIDE), BF16), dma((pieces,)), dma((pieces,)), dma((pieces,)),
        pltpu.VMEM((2 * tokens, 2 * kd), BF16), dma((2,)), dma((2,)),
        pltpu.VMEM((rows, half), BF16), dma, dma, dma,
        pltpu.VMEM((BLK, BLK), BF16), pltpu.VMEM((1, width), F32), pltpu.VMEM((1, width), F32), dma, dma,
        pltpu.VMEM((1, width), jnp.int32),
        pltpu.VMEM((pieces, 2 * tokens, WIDE), F32),
        strip(hop_buffers()), strip(hop_buffers()), dma((2, most, pieces)), dma((2, most, pieces)),
        pltpu.VMEM((nx, pieces, rows, WIDE), BF16), pltpu.VMEM((nx, pieces, rows, WIDE), BF16),
        dma((nx, pieces)), dma((nx, pieces)),
        pltpu.VMEM((2, 2, pieces, mine, WIDE), BF16), dma((2, 2, pieces)), dma((2, 2, pieces)),
        pltpu.VMEM((rows, WIDE), F32), pltpu.VMEM((pieces, mine, WIDE), F32),
        pltpu.VMEM((pieces, mine, WIDE), BF16), pltpu.VMEM((pieces, mine, WIDE), BF16),
        dma((pieces,)), dma((pieces,)),
        pltpu.VMEM((2, pieces, mine, WIDE), BF16), dma((2, pieces)),
    ]
    anywhere = pl.BlockSpec(memory_space=pltpu.HBM)
    return pl.pallas_call(
        kernel,
        out_shape=jax.ShapeDtypeStruct((1, mine, width), BF16),
        in_specs=[anywhere] * 10,
        out_specs=anywhere,
        scratch_shapes=scratch,
        compiler_params=pltpu.CompilerParams(
            collective_id=0, has_side_effects=True, vmem_limit_bytes=48 * 1024 * 1024),
        cost_estimate=pl.CostEstimate(
            flops=2 * 2 * tokens * kd * width, bytes_accessed=2 * kd * width, transcendentals=0),
    )(
        leave_query, leave_key, leave_value, arrive_query, arrive_key, arrive_value,
        leave_residual, out_weight, gate_scale, sign_bits.reshape(1, width),
    )


def solution(mesh):
    placed = (
        P("section", None, "tp"),
        P("section", None, "tp"),
        P("section", None, "tp"),
        P("section", None, "tp"),
        P("section", None, "tp"),
        P("section", None, "tp"),
        P("section", "tp", None),
        P("section", "tp", None),
        P("section", None),
        P(),
    )
    return jax.shard_map(
        local, mesh=mesh, in_specs=placed, out_specs=P("section", "tp", None), check_vma=False
    )
```

```python
import math

import jax
import jax.numpy as jnp
from jax import lax
from jax.experimental import pallas as pl
from jax.experimental.pallas import tpu as pltpu
from jax.sharding import PartitionSpec as P

HD = 128
BLK = 128
MESH = pl.DeviceIdType.MESH
F32 = jnp.float32
BF16 = jnp.bfloat16
WIDTHS = (1024, 1024, 1024)
FIRST = (4, 3)
MODES = (
    (("next", "next", "apart", "apart"), ("next", "back", "back")),
    (("next", "next", "apart", "apart"), ("next", "back", "back")),
    (("next", "next", "apart", "apart"), ("next", "back", "back")),
)
ORDER = (
    ("P", 2), ("A4", 2), ("cB3", 2), ("P", 1), ("cA1", 1), ("cB3", 1), ("A4", 1), ("cA1", 2), ("P", 0), ("A4", 0),
    ("cA1", 0), ("cB3", 0), ("cB2", 1), ("cO", 0), ("cO", 2), ("A3", 2), ("jB3", 2), ("cB2", 0), ("cB2", 2),
    ("cO", 1), ("jB3", 1), ("A3", 1), ("A3", 0), ("jB3", 0), ("cA2", 2), ("jO", 0), ("jB2", 1), ("jO", 2),
    ("cA2", 1), ("jB2", 2), ("jO", 1), ("cA2", 0), ("jB2", 0), ("jA2", 2), ("cB1", 1), ("cB1", 2), ("jA2", 1),
    ("jA2", 0), ("cB1", 0), ("jA1", 2), ("jB1", 1), ("jA1", 1), ("jB1", 2), ("jA1", 0), ("jB1", 0), ("F", 1),
    ("F", 2), ("F", 0),
)
PIECES = len(WIDTHS)
STARTS = tuple(sum(WIDTHS[:p]) for p in range(PIECES))


def mode(ch, j, p):
    return MODES[p][ch][j - 1]


def joints(p):
    return [(ch, j) for ch, first in enumerate(FIRST) for j in range(1, first + 1) if mode(ch, j, p) != "apart"]


def kernel(
    lq, lk, lv, aq, ak, av, residual, weight, gate, sign_bits,
    out,
    qkv, qkv_sem,
    wbuf, w_sem, w_send, w_recv,
    att, att_send, att_recv,
    resbuf, res_sem, res_send, res_recv,
    table, signs, gates, gate_sem, sign_sem, bits_v,
    sums,
    zs, zr, zs_sem, zr_sem,
    xs, xr, xs_sem, xr_sem,
    fin, fs_sem, fin_sem,
    own0, own_keep, own_s, own_r, os_sem, or_sem,
):
    sections = lax.axis_size("section")
    chips = lax.axis_size("tp") // 2
    s = lax.axis_index("section")
    tp = lax.axis_index("tp")
    z = tp >> 1
    c = tp & 1
    other = 1 - c
    tokens = lq.shape[1]
    kd = lq.shape[2]
    width = residual.shape[2]
    half = width // 2
    rows = tokens // chips
    mine = rows // 2

    def wrapped(at, count):
        return jnp.where(at < 0, at + count, jnp.where(at >= count, at - count, at))

    side = 1 - 2 * c
    around = {k: wrapped(z + k * side, chips) for k in range(-max(FIRST), max(FIRST) + 1)}
    row_of = {k: pl.multiple_of(rows * at, rows) for k, at in around.items()}
    near = {k: {"section": s, "tp": 2 * around[k] + c} for k in (-1, 1)}
    near_core = {(k, core): {"section": s, "tp": 2 * around[k] + core} for k in (-1, 1) for core in (0, 1)}
    next_section = {"section": wrapped(s + 1, sections), "tp": tp}
    prev_section = {"section": wrapped(s - 1, sections), "tp": tp}
    partner = {"section": s, "tp": 2 * z + other}

    barrier = pltpu.get_barrier_semaphore()
    greeted = [partner, next_section, prev_section] + list(near_core.values())
    for device in greeted:
        pl.semaphore_signal(barrier, inc=1, device_id=device, device_id_type=MESH)

    def toward(ch, p):
        return 1 if (ch + p) % 2 == 0 else -1

    def cols(p, which):
        return pl.ds(pl.multiple_of(which * half + STARTS[p], 128), WIDTHS[p])

    loads = []
    for i, ref in enumerate((lq, lk, lv, aq, ak, av)):
        loads.append(pltpu.make_async_copy(ref.at[0], qkv.at[i], qkv_sem.at[i]))
        loads[-1].start()

    def w_local(p):
        return pltpu.make_async_copy(weight.at[0, :, cols(p, c)], wbuf[p].at[pl.ds(0, kd)], w_sem.at[p])

    def w_remote(p):
        return pltpu.make_async_remote_copy(
            weight.at[0, :, cols(p, other)], wbuf[p].at[pl.ds(kd, kd)], w_send.at[p], w_recv.at[p],
            device_id=partner, device_id_type=MESH)

    for p in range(PIECES):
        w_local(p).start()
    gate_copy = pltpu.make_async_copy(gate, gates, gate_sem)
    gate_copy.start()
    sign_copy = pltpu.make_async_copy(sign_bits, bits_v, sign_sem)
    sign_copy.start()
    own_rows = pl.ds(pl.multiple_of(mine * c, mine), mine)
    other_rows = pl.ds(pl.multiple_of(mine * other, mine), mine)
    res_local = pltpu.make_async_copy(
        residual.at[0, :, pl.ds(pl.multiple_of(c * half, 128), half)], resbuf.at[own_rows], res_sem)
    res_local.start()

    pl.semaphore_wait(barrier, len(greeted))

    for p in range(PIECES):
        w_remote(p).start()
    res_remote = pltpu.make_async_remote_copy(
        residual.at[0, :, pl.ds(pl.multiple_of(other * half, 128), half)], resbuf.at[own_rows], res_send, res_recv,
        device_id=partner, device_id_type=MESH)
    res_remote.start()

    def att_copy(m):
        there = att.at[pl.ds(m * tokens, tokens), pl.ds(kd, kd)]
        here = att.at[pl.ds(m * tokens, tokens), pl.ds(0, kd)]
        return pltpu.make_async_remote_copy(
            here, there, att_send.at[m], att_recv.at[m], device_id=partner, device_id_type=MESH)

    for m in range(2):
        for i in range(3):
            loads[3 * m + i].wait()
        for h in range(kd // HD):
            lanes = pl.ds(h * HD, HD)
            query, key, value = (qkv[3 * m + i, :, lanes] for i in range(3))
            scores = lax.dot_general(query, key, (((1,), (1,)), ((), ())), preferred_element_type=F32)
            scores = scores * (1.0 / math.sqrt(HD))
            peak = jnp.max(scores, axis=-1, keepdims=True)
            raised = jnp.exp(scores - peak)
            probs = (raised / jnp.sum(raised, axis=-1, keepdims=True)).astype(BF16)
            mixed = jnp.dot(probs, value, preferred_element_type=F32)
            att[pl.ds(m * tokens, tokens), lanes] = mixed.astype(BF16)
        att_copy(m).start()

    i = lax.broadcasted_iota(jnp.int32, (BLK, BLK), 0)
    j = lax.broadcasted_iota(jnp.int32, (BLK, BLK), 1)
    anded = i & j
    anded = anded ^ (anded >> 4)
    anded = anded ^ (anded >> 2)
    anded = anded ^ (anded >> 1)
    table[...] = (1 - 2 * (anded & 1)).astype(F32).astype(BF16)
    sign_copy.wait()
    signs[...] = 1.0 - 2.0 * bits_v[...].astype(F32)

    def turned(values):
        r, n = values.shape[0], values.shape[1] // BLK
        blocks = jnp.concatenate([values[:, b * BLK:(b + 1) * BLK] for b in range(n)], axis=0)
        made = jnp.dot(blocks, table[...], preferred_element_type=F32)
        return jnp.concatenate([made[b * r:(b + 1) * r] for b in range(n)], axis=1)

    gate_copy.wait()
    res_local.wait()
    res_remote.wait_recv()
    for m in range(2):
        att_copy(m).wait_recv()

    def leaving(p, at):
        return sums[p][pl.ds(row_of[at], rows), :]

    def arriving(p, at):
        return sums[p][pl.ds(pl.multiple_of(tokens + row_of[at], rows), rows), :]

    def z_copy(ch, j, p):
        to = near[toward(ch, p)]
        return pltpu.make_async_remote_copy(
            zs[p][ch][j], zr[p][ch][j], zs_sem.at[ch, j, p], zr_sem.at[ch, j, p], device_id=to, device_id_type=MESH)

    def fin_copy(ch, core, p):
        to = near_core[toward(ch, p), core]
        return pltpu.make_async_remote_copy(
            zs[p][ch][1].at[pl.ds(core * mine, mine)], fin[p].at[ch, c],
            fs_sem.at[ch, core, p], fin_sem.at[ch, c, p], device_id=to, device_id_type=MESH)

    def fin_arrival(ch, core, p):
        return pltpu.make_async_remote_copy(
            zs[p][ch][1].at[pl.ds(0, mine)], fin[p].at[ch, core],
            fs_sem.at[ch, 0, p], fin_sem.at[ch, core, p], device_id=partner, device_id_type=MESH)

    def x_copy(at, p):
        to = next_section if at == 0 or mode(*joints(p)[at - 1], p) == "next" else prev_section
        return pltpu.make_async_remote_copy(
            xs[p].at[at], xr[p].at[at], xs_sem.at[at, p], xr_sem.at[at, p], device_id=to, device_id_type=MESH)

    def slot(ch, j, p):
        return joints(p).index((ch, j)) + 1

    def own_copy(p):
        return pltpu.make_async_remote_copy(
            own_s[p], own_r[p], os_sem.at[p], or_sem.at[p], device_id=partner, device_id_type=MESH)

    def target(ch, j, p):
        return j * toward(ch, p)

    def come(ch, j, p, arrived):
        kind = mode(ch, j + 1, p) if j < FIRST[ch] else None
        if kind == "apart":
            return zr[p][ch][j + 1][rows:] if arrived else zr[p][ch][j + 1][:rows]
        if kind == ("next" if arrived else "back"):
            return zr[p][ch][j + 1][...]
        return None

    def plus(sums_here, other_sums):
        return sums_here if other_sums is None else sums_here + other_sums.astype(F32)

    def apart(ch, j, p):
        if j < FIRST[ch]:
            z_copy(ch, j + 1, p).wait_recv()
        at = target(ch, j, p)
        zs[p][ch][j][:rows] = plus(leaving(p, at), come(ch, j, p, False)).astype(BF16)
        zs[p][ch][j][rows:] = plus(arriving(p, at), come(ch, j, p, True)).astype(BF16)
        z_copy(ch, j, p).start()

    def cross(ch, j, p):
        arrived = mode(ch, j, p) == "back"
        own = (arriving if arrived else leaving)(p, target(ch, j, p))
        if come(ch, j, p, arrived) is not None:
            z_copy(ch, j + 1, p).wait_recv()
        xs[p][slot(ch, j, p)] = plus(own, come(ch, j, p, arrived)).astype(BF16)
        x_copy(slot(ch, j, p), p).start()

    def joined(ch, j, p):
        arrived = mode(ch, j, p) == "next"
        own = (arriving if arrived else leaving)(p, target(ch, j, p))
        x_copy(slot(ch, j, p), p).wait_recv()
        own = own + xr[p][slot(ch, j, p)].astype(F32)
        if come(ch, j, p, arrived) is not None and come(ch, j, p, not arrived) is None:
            z_copy(ch, j + 1, p).wait_recv()
        zs[p][ch][j][...] = plus(own, come(ch, j, p, arrived)).astype(BF16)
        if j > 1:
            z_copy(ch, j, p).start()
        else:
            for core in (0, 1):
                fin_copy(ch, core, p).start()

    def own_cross(p):
        plain = turned(resbuf[:, pl.ds(STARTS[p], WIDTHS[p])])
        plain = plain * (signs[:, cols(p, c)] * (1.0 / math.sqrt(BLK)))
        xs[p][0] = (leaving(p, 0) + plain).astype(BF16)
        x_copy(0, p).start()

    def own_joined(p):
        x_copy(0, p).wait_recv()
        own0[p][...] = arriving(p, 0) + xr[p][0].astype(F32)
        own_keep[p][...] = own0[p][own_rows, :]
        own_s[p][...] = own0[p][other_rows, :].astype(BF16)
        own_copy(p).start()

    def project(p):
        w_local(p).wait()
        w_remote(p).wait_recv()
        made = jnp.dot(att[...], wbuf[p][...], preferred_element_type=F32)
        sums[p][...] = made * gates[:, cols(p, c)]

    def finish(p):
        w_remote(p).wait_send()
        for at in range(1 + len(joints(p))):
            x_copy(at, p).wait_send()
        for ch, first in enumerate(FIRST):
            for j in range(2, first + 1):
                z_copy(ch, j, p).wait_send()
        own_copy(p).wait()
        for ch in range(2):
            for core in (0, 1):
                fin_copy(ch, core, p).wait_send()
                fin_arrival(ch, core, p).wait_recv()
        for core, own in ((c, own_keep[p][...]), (other, own_r[p][...].astype(F32))):
            total = own + fin[p][0, core].astype(F32) + fin[p][1, core].astype(F32)
            total = total * signs[:, cols(p, core)]
            high = total.astype(BF16)
            low = (total - high.astype(F32)).astype(BF16)
            r = turned(jnp.concatenate([high, low], axis=0))
            r = (r[:mine] + r[mine:]) * (1.0 / math.sqrt(BLK))
            out[0, :, cols(p, core)] = r.astype(BF16)

    for step, p in ORDER:
        if step == "P":
            project(p)
        elif step == "F":
            finish(p)
        elif step == "cO":
            own_cross(p)
        elif step == "jO":
            own_joined(p)
        else:
            ch, j = "AB".index(step[-2]), int(step[-1])
            (cross if step[0] == "c" else joined if step[0] == "j" else apart)(ch, j, p)

    res_remote.wait_send()
    for m in range(2):
        att_copy(m).wait_send()


def local(
    leave_query, leave_key, leave_value, arrive_query, arrive_key, arrive_value,
    leave_residual, out_weight, gate_scale, sign_bits,
):
    tokens, kd = leave_query.shape[1:]
    width = leave_residual.shape[2]
    chips = lax.axis_size("tp") // 2
    rows, mine = tokens // chips, tokens // chips // 2
    half = width // 2
    dma = pltpu.SemaphoreType.DMA

    def each(shape, kind):
        return [pltpu.VMEM(shape + (w,), kind) for w in WIDTHS]

    def hops():
        return [
            [[pltpu.VMEM((2 * rows if j > 0 and mode(ch, j, p) == "apart" else rows, w), BF16) for j in range(first + 1)]
             for ch, first in enumerate(FIRST)]
            for p, w in enumerate(WIDTHS)
        ]

    def crossings():
        return [pltpu.VMEM((1 + len(joints(p)), rows, w), BF16) for p, w in enumerate(WIDTHS)]

    most = max(FIRST) + 1
    nx = 1 + max(len(joints(p)) for p in range(PIECES))
    scratch = [
        pltpu.VMEM((6, tokens, kd), BF16), dma((6,)),
        each((2 * kd,), BF16), dma((PIECES,)), dma((PIECES,)), dma((PIECES,)),
        pltpu.VMEM((2 * tokens, 2 * kd), BF16), dma((2,)), dma((2,)),
        pltpu.VMEM((rows, half), BF16), dma, dma, dma,
        pltpu.VMEM((BLK, BLK), BF16), pltpu.VMEM((1, width), F32), pltpu.VMEM((1, width), F32), dma, dma,
        pltpu.VMEM((1, width), jnp.int32),
        each((2 * tokens,), F32),
        hops(), hops(), dma((2, most, PIECES)), dma((2, most, PIECES)),
        crossings(), crossings(), dma((nx, PIECES)), dma((nx, PIECES)),
        each((2, 2, mine), BF16), dma((2, 2, PIECES)), dma((2, 2, PIECES)),
        each((rows,), F32), each((mine,), F32), each((mine,), BF16), each((mine,), BF16),
        dma((PIECES,)), dma((PIECES,)),
    ]
    operands = (
        leave_query, leave_key, leave_value, arrive_query, arrive_key, arrive_value,
        leave_residual, out_weight, gate_scale, sign_bits.reshape(1, width),
    )
    return pl.pallas_call(
        kernel,
        out_shape=pltpu.VMEM((1, mine, width), BF16),
        in_specs=[pl.BlockSpec(memory_space=pltpu.HBM)] * len(operands),
        out_specs=pl.BlockSpec(memory_space=pltpu.VMEM),
        scratch_shapes=scratch,
        compiler_params=pltpu.CompilerParams(
            collective_id=0, has_side_effects=True, vmem_limit_bytes=48 * 1024 * 1024),
        cost_estimate=pl.CostEstimate(
            flops=2 * 2 * tokens * kd * width, bytes_accessed=2 * kd * width, transcendentals=0),
    )(*(pltpu.with_memory_space_constraint(x, pltpu.HBM) for x in operands))


def solution(mesh):
    placed = (
        P("section", None, "tp"),
        P("section", None, "tp"),
        P("section", None, "tp"),
        P("section", None, "tp"),
        P("section", None, "tp"),
        P("section", None, "tp"),
        P("section", "tp", None),
        P("section", "tp", None),
        P("section", None),
        P(),
    )
    return jax.shard_map(
        local, mesh=mesh, in_specs=placed, out_specs=P("section", "tp", None), check_vma=False
    )
```

```python
import math

import jax
import jax.numpy as jnp
from jax import lax
from jax.experimental import pallas as pl
from jax.experimental.pallas import tpu as pltpu
from jax.sharding import PartitionSpec as P

HD = 128
BLK = 128
MESH = pl.DeviceIdType.MESH
F32 = jnp.float32
BF16 = jnp.bfloat16
WIDTHS = (768, 1280, 1024)
FIRST = (4, 3)
MODES = (
    (("next", "next", "apart", "apart"), ("next", "back", "back")),
    (("next", "next", "apart", "apart"), ("next", "back", "back")),
    (("next", "next", "apart", "apart"), ("next", "back", "back")),
)
ORDER = (
    ("P", 0), ("cB3", 0), ("A4", 0), ("cA1", 0), ("P", 1), ("A4", 1), ("cO", 0), ("P", 2), ("cB3", 1), ("A4", 2),
    ("cA1", 2), ("cO", 1), ("cB2", 0), ("jB3", 0), ("cB3", 2), ("A3", 0), ("cA1", 1), ("cB2", 1), ("A3", 1),
    ("jB3", 1), ("cO", 2), ("cB2", 2), ("A3", 2), ("jB3", 2), ("cA2", 0), ("jO", 0), ("jB2", 0), ("jO", 1),
    ("cA2", 1), ("jB2", 1), ("cA2", 2), ("jB2", 2), ("cB1", 0), ("cB1", 1), ("jA2", 0), ("jA2", 1), ("jA2", 2),
    ("jO", 2), ("cB1", 2), ("jB1", 0), ("jA1", 0), ("jA1", 1), ("jB1", 1), ("jA1", 2), ("jB1", 2), ("F", 0),
    ("F", 1), ("F", 2),
)
PIECES = len(WIDTHS)
STARTS = tuple(sum(WIDTHS[:p]) for p in range(PIECES))


def mode(ch, j, p):
    return MODES[p][ch][j - 1]


def joints(p):
    return [(ch, j) for ch, first in enumerate(FIRST) for j in range(1, first + 1) if mode(ch, j, p) != "apart"]


def kernel(
    lq, lk, lv, aq, ak, av, residual, weight, gate, sign_bits,
    out,
    qkv, qkv_sem,
    wbuf, w_sem, w_send, w_recv, wahead, ahead_sem,
    att, att_send, att_recv,
    resbuf, res_sem, res_send, res_recv,
    table, signs, gates, gate_sem, sign_sem, bits_v,
    sums,
    zs, zr, zs_sem, zr_sem,
    xs, xr, xs_sem, xr_sem,
    fin, fs_sem, fin_sem,
    own0, own_keep, own_s, own_r, os_sem, or_sem,
):
    sections = lax.axis_size("section")
    chips = lax.axis_size("tp") // 2
    s = lax.axis_index("section")
    tp = lax.axis_index("tp")
    z = tp >> 1
    c = tp & 1
    other = 1 - c
    tokens = lq.shape[1]
    kd = lq.shape[2]
    width = residual.shape[2]
    half = width // 2
    rows = tokens // chips
    mine = rows // 2

    def wrapped(at, count):
        return jnp.where(at < 0, at + count, jnp.where(at >= count, at - count, at))

    side = 1 - 2 * c
    around = {k: wrapped(z + k * side, chips) for k in range(-max(FIRST), max(FIRST) + 1)}
    row_of = {k: pl.multiple_of(rows * at, rows) for k, at in around.items()}
    near = {k: {"section": s, "tp": 2 * around[k] + c} for k in (-1, 1)}
    near_core = {(k, core): {"section": s, "tp": 2 * around[k] + core} for k in (-1, 1) for core in (0, 1)}
    next_section = {"section": wrapped(s + 1, sections), "tp": tp}
    prev_section = {"section": wrapped(s - 1, sections), "tp": tp}
    partner = {"section": s, "tp": 2 * z + other}

    barrier = pltpu.get_barrier_semaphore()
    greeted = [partner, next_section, prev_section] + list(near_core.values())
    for device in greeted:
        pl.semaphore_signal(barrier, inc=1, device_id=device, device_id_type=MESH)

    def toward(ch, p):
        return 1 if (ch + p) % 2 == 0 else -1

    def cols(p, which):
        return pl.ds(pl.multiple_of(which * half + STARTS[p], 128), WIDTHS[p])

    loads = []
    for i, ref in enumerate((lq, lk, lv, aq, ak, av)):
        loads.append(pltpu.make_async_copy(ref.at[0], qkv.at[i], qkv_sem.at[i]))
        loads[-1].start()

    def w_local(p):
        return pltpu.make_async_copy(weight.at[0, :, cols(p, c)], wbuf[p].at[pl.ds(0, kd)], w_sem.at[p])

    def w_ahead(p):
        return pltpu.make_async_copy(weight.at[0, :, cols(p, other)], wahead[p], ahead_sem.at[p])

    def send_weights(p):
        w_ahead(p).wait()
        w_remote(p).start()

    def w_remote(p):
        return pltpu.make_async_remote_copy(
            wahead[p], wbuf[p].at[pl.ds(kd, kd)], w_send.at[p], w_recv.at[p],
            device_id=partner, device_id_type=MESH)

    for p in range(PIECES):
        w_ahead(p).start()
    for p in range(PIECES):
        w_local(p).start()
    gate_copy = pltpu.make_async_copy(gate, gates, gate_sem)
    gate_copy.start()
    sign_copy = pltpu.make_async_copy(sign_bits, bits_v, sign_sem)
    sign_copy.start()
    own_rows = pl.ds(pl.multiple_of(mine * c, mine), mine)
    other_rows = pl.ds(pl.multiple_of(mine * other, mine), mine)
    res_local = pltpu.make_async_copy(
        residual.at[0, :, pl.ds(pl.multiple_of(c * half, 128), half)], resbuf.at[own_rows], res_sem)
    res_local.start()

    pl.semaphore_wait(barrier, len(greeted))

    res_remote = pltpu.make_async_remote_copy(
        residual.at[0, :, pl.ds(pl.multiple_of(other * half, 128), half)], resbuf.at[own_rows], res_send, res_recv,
        device_id=partner, device_id_type=MESH)
    res_remote.start()
    send_weights(0)

    def att_copy(m):
        there = att.at[pl.ds(m * tokens, tokens), pl.ds(kd, kd)]
        here = att.at[pl.ds(m * tokens, tokens), pl.ds(0, kd)]
        return pltpu.make_async_remote_copy(
            here, there, att_send.at[m], att_recv.at[m], device_id=partner, device_id_type=MESH)

    for m in range(2):
        for i in range(3):
            loads[3 * m + i].wait()
        for h in range(kd // HD):
            lanes = pl.ds(h * HD, HD)
            query, key, value = (qkv[3 * m + i, :, lanes] for i in range(3))
            scores = lax.dot_general(query, key, (((1,), (1,)), ((), ())), preferred_element_type=F32)
            scores = scores * (1.0 / math.sqrt(HD))
            peak = jnp.max(scores, axis=-1, keepdims=True)
            raised = jnp.exp(scores - peak)
            probs = (raised / jnp.sum(raised, axis=-1, keepdims=True)).astype(BF16)
            mixed = jnp.dot(probs, value, preferred_element_type=F32)
            att[pl.ds(m * tokens, tokens), lanes] = mixed.astype(BF16)
        att_copy(m).start()
    for p in range(1, PIECES):
        send_weights(p)

    i = lax.broadcasted_iota(jnp.int32, (BLK, BLK), 0)
    j = lax.broadcasted_iota(jnp.int32, (BLK, BLK), 1)
    anded = i & j
    anded = anded ^ (anded >> 4)
    anded = anded ^ (anded >> 2)
    anded = anded ^ (anded >> 1)
    table[...] = (1 - 2 * (anded & 1)).astype(F32).astype(BF16)
    sign_copy.wait()
    signs[...] = 1.0 - 2.0 * bits_v[...].astype(F32)

    def turned(values):
        r, n = values.shape[0], values.shape[1] // BLK
        blocks = jnp.concatenate([values[:, b * BLK:(b + 1) * BLK] for b in range(n)], axis=0)
        made = jnp.dot(blocks, table[...], preferred_element_type=F32)
        return jnp.concatenate([made[b * r:(b + 1) * r] for b in range(n)], axis=1)

    gate_copy.wait()
    for m in range(2):
        att_copy(m).wait_recv()

    def leaving(p, at):
        return sums[p][pl.ds(row_of[at], rows), :]

    def arriving(p, at):
        return sums[p][pl.ds(pl.multiple_of(tokens + row_of[at], rows), rows), :]

    def z_copy(ch, j, p):
        to = near[toward(ch, p)]
        return pltpu.make_async_remote_copy(
            zs[p][ch][j], zr[p][ch][j], zs_sem.at[ch, j, p], zr_sem.at[ch, j, p], device_id=to, device_id_type=MESH)

    def fin_copy(ch, core, p):
        to = near_core[toward(ch, p), core]
        return pltpu.make_async_remote_copy(
            zs[p][ch][1].at[pl.ds(core * mine, mine)], fin[p].at[ch, c],
            fs_sem.at[ch, core, p], fin_sem.at[ch, c, p], device_id=to, device_id_type=MESH)

    def fin_arrival(ch, core, p):
        return pltpu.make_async_remote_copy(
            zs[p][ch][1].at[pl.ds(0, mine)], fin[p].at[ch, core],
            fs_sem.at[ch, 0, p], fin_sem.at[ch, core, p], device_id=partner, device_id_type=MESH)

    def x_copy(at, p):
        to = next_section if at == 0 or mode(*joints(p)[at - 1], p) == "next" else prev_section
        return pltpu.make_async_remote_copy(
            xs[p].at[at], xr[p].at[at], xs_sem.at[at, p], xr_sem.at[at, p], device_id=to, device_id_type=MESH)

    def slot(ch, j, p):
        return joints(p).index((ch, j)) + 1

    def own_copy(p):
        return pltpu.make_async_remote_copy(
            own_s[p], own_r[p], os_sem.at[p], or_sem.at[p], device_id=partner, device_id_type=MESH)

    def target(ch, j, p):
        return j * toward(ch, p)

    def come(ch, j, p, arrived):
        kind = mode(ch, j + 1, p) if j < FIRST[ch] else None
        if kind == "apart":
            return zr[p][ch][j + 1][rows:] if arrived else zr[p][ch][j + 1][:rows]
        if kind == ("next" if arrived else "back"):
            return zr[p][ch][j + 1][...]
        return None

    def plus(sums_here, other_sums):
        return sums_here if other_sums is None else sums_here + other_sums.astype(F32)

    def apart(ch, j, p):
        if j < FIRST[ch]:
            z_copy(ch, j + 1, p).wait_recv()
        at = target(ch, j, p)
        zs[p][ch][j][:rows] = plus(leaving(p, at), come(ch, j, p, False)).astype(BF16)
        zs[p][ch][j][rows:] = plus(arriving(p, at), come(ch, j, p, True)).astype(BF16)
        z_copy(ch, j, p).start()

    def cross(ch, j, p):
        arrived = mode(ch, j, p) == "back"
        own = (arriving if arrived else leaving)(p, target(ch, j, p))
        if come(ch, j, p, arrived) is not None:
            z_copy(ch, j + 1, p).wait_recv()
        xs[p][slot(ch, j, p)] = plus(own, come(ch, j, p, arrived)).astype(BF16)
        x_copy(slot(ch, j, p), p).start()

    def joined(ch, j, p):
        arrived = mode(ch, j, p) == "next"
        own = (arriving if arrived else leaving)(p, target(ch, j, p))
        x_copy(slot(ch, j, p), p).wait_recv()
        own = own + xr[p][slot(ch, j, p)].astype(F32)
        if come(ch, j, p, arrived) is not None and come(ch, j, p, not arrived) is None:
            z_copy(ch, j + 1, p).wait_recv()
        zs[p][ch][j][...] = plus(own, come(ch, j, p, arrived)).astype(BF16)
        if j > 1:
            z_copy(ch, j, p).start()
        else:
            for core in (0, 1):
                fin_copy(ch, core, p).start()

    def own_cross(p):
        if p == ORDER[[step for step, _ in ORDER].index("cO")][1]:
            res_local.wait()
            res_remote.wait_recv()
        plain = turned(resbuf[:, pl.ds(STARTS[p], WIDTHS[p])])
        plain = plain * (signs[:, cols(p, c)] * (1.0 / math.sqrt(BLK)))
        xs[p][0] = (leaving(p, 0) + plain).astype(BF16)
        x_copy(0, p).start()

    def own_joined(p):
        x_copy(0, p).wait_recv()
        own0[p][...] = arriving(p, 0) + xr[p][0].astype(F32)
        own_keep[p][...] = own0[p][own_rows, :]
        own_s[p][...] = own0[p][other_rows, :].astype(BF16)
        own_copy(p).start()

    def project(p):
        w_local(p).wait()
        w_remote(p).wait_recv()
        made = jnp.dot(att[...], wbuf[p][...], preferred_element_type=F32)
        sums[p][...] = made * gates[:, cols(p, c)]

    def finish(p):
        w_remote(p).wait_send()
        for at in range(1 + len(joints(p))):
            x_copy(at, p).wait_send()
        for ch, first in enumerate(FIRST):
            for j in range(2, first + 1):
                z_copy(ch, j, p).wait_send()
        own_copy(p).wait()
        for ch in range(2):
            for core in (0, 1):
                fin_copy(ch, core, p).wait_send()
                fin_arrival(ch, core, p).wait_recv()
        for core, own in ((c, own_keep[p][...]), (other, own_r[p][...].astype(F32))):
            total = own + fin[p][0, core].astype(F32) + fin[p][1, core].astype(F32)
            total = total * signs[:, cols(p, core)]
            high = total.astype(BF16)
            low = (total - high.astype(F32)).astype(BF16)
            r = turned(jnp.concatenate([high, low], axis=0))
            r = (r[:mine] + r[mine:]) * (1.0 / math.sqrt(BLK))
            out[0, :, cols(p, core)] = r.astype(BF16)

    for step, p in ORDER:
        if step == "P":
            project(p)
        elif step == "F":
            finish(p)
        elif step == "cO":
            own_cross(p)
        elif step == "jO":
            own_joined(p)
        else:
            ch, j = "AB".index(step[-2]), int(step[-1])
            (cross if step[0] == "c" else joined if step[0] == "j" else apart)(ch, j, p)

    res_remote.wait_send()
    for m in range(2):
        att_copy(m).wait_send()


def local(
    leave_query, leave_key, leave_value, arrive_query, arrive_key, arrive_value,
    leave_residual, out_weight, gate_scale, sign_bits,
):
    tokens, kd = leave_query.shape[1:]
    width = leave_residual.shape[2]
    chips = lax.axis_size("tp") // 2
    rows, mine = tokens // chips, tokens // chips // 2
    half = width // 2
    dma = pltpu.SemaphoreType.DMA

    def each(shape, kind):
        return [pltpu.VMEM(shape + (w,), kind) for w in WIDTHS]

    def hops():
        return [
            [[pltpu.VMEM((2 * rows if j > 0 and mode(ch, j, p) == "apart" else rows, w), BF16) for j in range(first + 1)]
             for ch, first in enumerate(FIRST)]
            for p, w in enumerate(WIDTHS)
        ]

    def crossings():
        return [pltpu.VMEM((1 + len(joints(p)), rows, w), BF16) for p, w in enumerate(WIDTHS)]

    most = max(FIRST) + 1
    nx = 1 + max(len(joints(p)) for p in range(PIECES))
    scratch = [
        pltpu.VMEM((6, tokens, kd), BF16), dma((6,)),
        each((2 * kd,), BF16), dma((PIECES,)), dma((PIECES,)), dma((PIECES,)), each((kd,), BF16), dma((PIECES,)),
        pltpu.VMEM((2 * tokens, 2 * kd), BF16), dma((2,)), dma((2,)),
        pltpu.VMEM((rows, half), BF16), dma, dma, dma,
        pltpu.VMEM((BLK, BLK), BF16), pltpu.VMEM((1, width), F32), pltpu.VMEM((1, width), F32), dma, dma,
        pltpu.VMEM((1, width), jnp.int32),
        each((2 * tokens,), F32),
        hops(), hops(), dma((2, most, PIECES)), dma((2, most, PIECES)),
        crossings(), crossings(), dma((nx, PIECES)), dma((nx, PIECES)),
        each((2, 2, mine), BF16), dma((2, 2, PIECES)), dma((2, 2, PIECES)),
        each((rows,), F32), each((mine,), F32), each((mine,), BF16), each((mine,), BF16),
        dma((PIECES,)), dma((PIECES,)),
    ]
    operands = (
        leave_query, leave_key, leave_value, arrive_query, arrive_key, arrive_value,
        leave_residual, out_weight, gate_scale, sign_bits.reshape(1, width),
    )
    return pl.pallas_call(
        kernel,
        out_shape=pltpu.VMEM((1, mine, width), BF16),
        in_specs=[pl.BlockSpec(memory_space=pltpu.HBM)] * len(operands),
        out_specs=pl.BlockSpec(memory_space=pltpu.VMEM),
        scratch_shapes=scratch,
        compiler_params=pltpu.CompilerParams(
            collective_id=0, has_side_effects=True, vmem_limit_bytes=48 * 1024 * 1024),
        cost_estimate=pl.CostEstimate(
            flops=2 * 2 * tokens * kd * width, bytes_accessed=2 * kd * width, transcendentals=0),
    )(*(pltpu.with_memory_space_constraint(x, pltpu.HBM) for x in operands))


def solution(mesh):
    placed = (
        P("section", None, "tp"),
        P("section", None, "tp"),
        P("section", None, "tp"),
        P("section", None, "tp"),
        P("section", None, "tp"),
        P("section", None, "tp"),
        P("section", "tp", None),
        P("section", "tp", None),
        P("section", None),
        P(),
    )
    return jax.shard_map(
        local, mesh=mesh, in_specs=placed, out_specs=P("section", "tp", None), check_vma=False
    )
```

```python
import math

import jax
import jax.numpy as jnp
from jax import lax
from jax.experimental import pallas as pl
from jax.experimental.pallas import tpu as pltpu
from jax.sharding import PartitionSpec as P

HD = 128
BLK = 128
MESH = pl.DeviceIdType.MESH
F32 = jnp.float32
BF16 = jnp.bfloat16
WIDTHS = (768, 1280, 1024)
FIRST = (4, 3)
MODES = (
    (("next", "next", "apart", "apart"), ("next", "back", "back")),
    (("next", "next", "apart", "apart"), ("next", "back", "back")),
    (("next", "next", "apart", "apart"), ("next", "back", "back")),
)
ORDER = (
    ("P", 0), ("cB3", 0), ("A4", 0), ("cA1", 0), ("P", 1), ("A4", 1), ("cO", 0), ("P", 2), ("cB3", 1), ("A4", 2),
    ("cA1", 2), ("cO", 1), ("cB2", 0), ("jB3", 0), ("cB3", 2), ("A3", 0), ("cA1", 1), ("cB2", 1), ("A3", 1),
    ("jB3", 1), ("cO", 2), ("cB2", 2), ("A3", 2), ("jB3", 2), ("cA2", 0), ("jO", 0), ("jB2", 0), ("jO", 1),
    ("cA2", 1), ("jB2", 1), ("cA2", 2), ("jB2", 2), ("cB1", 0), ("cB1", 1), ("jA2", 0), ("jA2", 1), ("jA2", 2),
    ("jO", 2), ("cB1", 2), ("jB1", 0), ("jA1", 0), ("jA1", 1), ("jB1", 1), ("jA1", 2), ("jB1", 2), ("F", 0),
    ("F", 1), ("F", 2),
)
PIECES = len(WIDTHS)
STARTS = tuple(sum(WIDTHS[:p]) for p in range(PIECES))


def mode(ch, j, p):
    return MODES[p][ch][j - 1]


def joints(p):
    return [(ch, j) for ch, first in enumerate(FIRST) for j in range(1, first + 1) if mode(ch, j, p) != "apart"]


def kernel(
    lq, lk, lv, aq, ak, av, residual, weight, gate, sign_bits,
    out,
    qkv, qkv_sem,
    wbuf, w_sem, w_send, w_recv, wahead, ahead_sem,
    att, att_send, att_recv,
    resbuf, res_sem, res_send, res_recv,
    table, signs, gates, gate_sem, sign_sem, bits_v,
    sums,
    zs, zr, zr_sem,
    xs, xr, xr_sem,
    fin, fin_sem, sent,
    own0, own_keep, own_s, own_r, or_sem,
):
    sections = lax.axis_size("section")
    chips = lax.axis_size("tp") // 2
    s = lax.axis_index("section")
    tp = lax.axis_index("tp")
    z = tp >> 1
    c = tp & 1
    other = 1 - c
    tokens = lq.shape[1]
    kd = lq.shape[2]
    width = residual.shape[2]
    half = width // 2
    rows = tokens // chips
    mine = rows // 2

    def wrapped(at, count):
        return jnp.where(at < 0, at + count, jnp.where(at >= count, at - count, at))

    side = 1 - 2 * c
    around = {k: wrapped(z + k * side, chips) for k in range(-max(FIRST), max(FIRST) + 1)}
    row_of = {k: pl.multiple_of(rows * at, rows) for k, at in around.items()}
    near = {k: {"section": s, "tp": 2 * around[k] + c} for k in (-1, 1)}
    near_core = {(k, core): {"section": s, "tp": 2 * around[k] + core} for k in (-1, 1) for core in (0, 1)}
    next_section = {"section": wrapped(s + 1, sections), "tp": tp}
    prev_section = {"section": wrapped(s - 1, sections), "tp": tp}
    partner = {"section": s, "tp": 2 * z + other}

    barrier = pltpu.get_barrier_semaphore()
    greeted = [partner, next_section, prev_section] + list(near_core.values())
    for device in greeted:
        pl.semaphore_signal(barrier, inc=1, device_id=device, device_id_type=MESH)

    def toward(ch, p):
        return 1 if (ch + p) % 2 == 0 else -1

    def cols(p, which):
        return pl.ds(pl.multiple_of(which * half + STARTS[p], 128), WIDTHS[p])

    loads = []
    for i, ref in enumerate((lq, lk, lv, aq, ak, av)):
        loads.append(pltpu.make_async_copy(ref.at[0], qkv.at[i], qkv_sem.at[i]))
        loads[-1].start()

    def w_local(p):
        return pltpu.make_async_copy(weight.at[0, :, cols(p, c)], wbuf[p].at[pl.ds(0, kd)], w_sem.at[p])

    def w_ahead(p):
        return pltpu.make_async_copy(weight.at[0, :, cols(p, other)], wahead[p], ahead_sem.at[p])

    def send_weights(p):
        w_ahead(p).wait()
        w_remote(p).start()

    def w_remote(p):
        return pltpu.make_async_remote_copy(
            wahead[p], wbuf[p].at[pl.ds(kd, kd)], w_send.at[p], w_recv.at[p],
            device_id=partner, device_id_type=MESH)

    for p in range(PIECES):
        w_ahead(p).start()
    for p in range(PIECES):
        w_local(p).start()
    gate_copy = pltpu.make_async_copy(gate, gates, gate_sem)
    gate_copy.start()
    sign_copy = pltpu.make_async_copy(sign_bits, bits_v, sign_sem)
    sign_copy.start()
    own_rows = pl.ds(pl.multiple_of(mine * c, mine), mine)
    other_rows = pl.ds(pl.multiple_of(mine * other, mine), mine)
    res_local = pltpu.make_async_copy(
        residual.at[0, :, pl.ds(pl.multiple_of(c * half, 128), half)], resbuf.at[own_rows], res_sem)
    res_local.start()

    pl.semaphore_wait(barrier, len(greeted))

    res_remote = pltpu.make_async_remote_copy(
        residual.at[0, :, pl.ds(pl.multiple_of(other * half, 128), half)], resbuf.at[own_rows], res_send, res_recv,
        device_id=partner, device_id_type=MESH)
    res_remote.start()
    send_weights(0)

    def att_copy(m):
        there = att.at[pl.ds(m * tokens, tokens), pl.ds(kd, kd)]
        here = att.at[pl.ds(m * tokens, tokens), pl.ds(0, kd)]
        return pltpu.make_async_remote_copy(
            here, there, att_send.at[m], att_recv.at[m], device_id=partner, device_id_type=MESH)

    for m in range(2):
        for i in range(3):
            loads[3 * m + i].wait()
        for h in range(kd // HD):
            lanes = pl.ds(h * HD, HD)
            query, key, value = (qkv[3 * m + i, :, lanes] for i in range(3))
            scores = lax.dot_general(query, key, (((1,), (1,)), ((), ())), preferred_element_type=F32)
            scores = scores * (1.0 / math.sqrt(HD))
            peak = jnp.max(scores, axis=-1, keepdims=True)
            raised = jnp.exp(scores - peak)
            probs = (raised / jnp.sum(raised, axis=-1, keepdims=True)).astype(BF16)
            mixed = jnp.dot(probs, value, preferred_element_type=F32)
            att[pl.ds(m * tokens, tokens), lanes] = mixed.astype(BF16)
        att_copy(m).start()
    for p in range(1, PIECES):
        send_weights(p)

    i = lax.broadcasted_iota(jnp.int32, (BLK, BLK), 0)
    j = lax.broadcasted_iota(jnp.int32, (BLK, BLK), 1)
    anded = i & j
    anded = anded ^ (anded >> 4)
    anded = anded ^ (anded >> 2)
    anded = anded ^ (anded >> 1)
    table[...] = (1 - 2 * (anded & 1)).astype(F32).astype(BF16)
    sign_copy.wait()
    signs[...] = 1.0 - 2.0 * bits_v[...].astype(F32)

    def turned(values):
        r, n = values.shape[0], values.shape[1] // BLK
        blocks = jnp.concatenate([values[:, b * BLK:(b + 1) * BLK] for b in range(n)], axis=0)
        made = jnp.dot(blocks, table[...], preferred_element_type=F32)
        return jnp.concatenate([made[b * r:(b + 1) * r] for b in range(n)], axis=1)

    gate_copy.wait()

    def leaving(p, at):
        return sums[p][pl.ds(row_of[at], rows), :]

    def arriving(p, at):
        return sums[p][pl.ds(pl.multiple_of(tokens + row_of[at], rows), rows), :]

    def z_copy(ch, j, p):
        to = near[toward(ch, p)]
        return pltpu.make_async_remote_copy(
            zs[p][ch][j], zr[p][ch][j], sent.at[p], zr_sem.at[ch, j, p], device_id=to, device_id_type=MESH)

    def fin_copy(ch, core, p):
        to = near_core[toward(ch, p), core]
        return pltpu.make_async_remote_copy(
            zs[p][ch][1].at[pl.ds(core * mine, mine)], fin[p].at[ch, c],
            sent.at[p], fin_sem.at[ch, c, p], device_id=to, device_id_type=MESH)

    def fin_arrival(ch, core, p):
        return pltpu.make_async_remote_copy(
            zs[p][ch][1].at[pl.ds(0, mine)], fin[p].at[ch, core],
            sent.at[p], fin_sem.at[ch, core, p], device_id=partner, device_id_type=MESH)

    def x_copy(at, p):
        to = next_section if at == 0 or mode(*joints(p)[at - 1], p) == "next" else prev_section
        return pltpu.make_async_remote_copy(
            xs[p].at[at], xr[p].at[at], sent.at[p], xr_sem.at[at, p], device_id=to, device_id_type=MESH)

    def slot(ch, j, p):
        return joints(p).index((ch, j)) + 1

    def own_copy(p):
        return pltpu.make_async_remote_copy(
            own_s[p], own_r[p], sent.at[p], or_sem.at[p], device_id=partner, device_id_type=MESH)

    def target(ch, j, p):
        return j * toward(ch, p)

    def come(ch, j, p, arrived):
        kind = mode(ch, j + 1, p) if j < FIRST[ch] else None
        if kind == "apart":
            return zr[p][ch][j + 1][rows:] if arrived else zr[p][ch][j + 1][:rows]
        if kind == ("next" if arrived else "back"):
            return zr[p][ch][j + 1][...]
        return None

    def plus(sums_here, other_sums):
        return sums_here if other_sums is None else sums_here + other_sums.astype(F32)

    def apart(ch, j, p):
        if j < FIRST[ch]:
            z_copy(ch, j + 1, p).wait_recv()
        at = target(ch, j, p)
        zs[p][ch][j][:rows] = plus(leaving(p, at), come(ch, j, p, False)).astype(BF16)
        zs[p][ch][j][rows:] = plus(arriving(p, at), come(ch, j, p, True)).astype(BF16)
        z_copy(ch, j, p).start()

    def cross(ch, j, p):
        arrived = mode(ch, j, p) == "back"
        own = (arriving if arrived else leaving)(p, target(ch, j, p))
        if come(ch, j, p, arrived) is not None:
            z_copy(ch, j + 1, p).wait_recv()
        xs[p][slot(ch, j, p)] = plus(own, come(ch, j, p, arrived)).astype(BF16)
        x_copy(slot(ch, j, p), p).start()

    def joined(ch, j, p):
        arrived = mode(ch, j, p) == "next"
        own = (arriving if arrived else leaving)(p, target(ch, j, p))
        x_copy(slot(ch, j, p), p).wait_recv()
        own = own + xr[p][slot(ch, j, p)].astype(F32)
        if come(ch, j, p, arrived) is not None and come(ch, j, p, not arrived) is None:
            z_copy(ch, j + 1, p).wait_recv()
        zs[p][ch][j][...] = plus(own, come(ch, j, p, arrived)).astype(BF16)
        if j > 1:
            z_copy(ch, j, p).start()
        else:
            for core in (0, 1):
                fin_copy(ch, core, p).start()

    def own_cross(p):
        if p == ORDER[[step for step, _ in ORDER].index("cO")][1]:
            res_local.wait()
            res_remote.wait_recv()
        plain = turned(resbuf[:, pl.ds(STARTS[p], WIDTHS[p])])
        plain = plain * (signs[:, cols(p, c)] * (1.0 / math.sqrt(BLK)))
        xs[p][0] = (leaving(p, 0) + plain).astype(BF16)
        x_copy(0, p).start()

    def own_joined(p):
        x_copy(0, p).wait_recv()
        own0[p][...] = arriving(p, 0) + xr[p][0].astype(F32)
        own_keep[p][...] = own0[p][own_rows, :]
        own_s[p][...] = own0[p][other_rows, :].astype(BF16)
        own_copy(p).start()

    def project(p):
        if p > 0:
            w_local(p).wait()
            w_remote(p).wait_recv()
            made = jnp.dot(att[...], wbuf[p][...], preferred_element_type=F32)
            sums[p][...] = made * gates[:, cols(p, c)]
            return
        w_local(p).wait()
        sums[p][...] = jnp.dot(att[:, :kd], wbuf[p][:kd], preferred_element_type=F32)
        for m in range(2):
            att_copy(m).wait_recv()
        w_remote(p).wait_recv()
        made = sums[p][...] + jnp.dot(att[:, kd:], wbuf[p][kd:], preferred_element_type=F32)
        sums[p][...] = made * gates[:, cols(p, c)]

    def finish(p):
        own_copy(p).wait_recv()
        for ch in range(2):
            for core in (0, 1):
                fin_arrival(ch, core, p).wait_recv()
        for core, own in ((c, own_keep[p][...]), (other, own_r[p][...].astype(F32))):
            total = own + fin[p][0, core].astype(F32) + fin[p][1, core].astype(F32)
            total = total * signs[:, cols(p, core)]
            high = total.astype(BF16)
            low = (total - high.astype(F32)).astype(BF16)
            r = turned(jnp.concatenate([high, low], axis=0))
            r = (r[:mine] + r[mine:]) * (1.0 / math.sqrt(BLK))
            out[0, :, cols(p, core)] = r.astype(BF16)

    for step, p in ORDER:
        if step == "P":
            project(p)
        elif step == "F":
            finish(p)
        elif step == "cO":
            own_cross(p)
        elif step == "jO":
            own_joined(p)
        else:
            ch, j = "AB".index(step[-2]), int(step[-1])
            (cross if step[0] == "c" else joined if step[0] == "j" else apart)(ch, j, p)

    res_remote.wait_send()
    for m in range(2):
        att_copy(m).wait_send()
    for p in range(PIECES):
        w_remote(p).wait_send()
        count = mine + rows * (1 + len(joints(p)) + len(FIRST))
        for ch, first in enumerate(FIRST):
            count += sum(zs[p][ch][j].shape[0] for j in range(2, first + 1))
        whole = wbuf[p].at[pl.ds(0, count)]
        pltpu.make_async_copy(whole, whole, sent.at[p]).wait()


def local(
    leave_query, leave_key, leave_value, arrive_query, arrive_key, arrive_value,
    leave_residual, out_weight, gate_scale, sign_bits,
):
    tokens, kd = leave_query.shape[1:]
    width = leave_residual.shape[2]
    chips = lax.axis_size("tp") // 2
    rows, mine = tokens // chips, tokens // chips // 2
    half = width // 2
    dma = pltpu.SemaphoreType.DMA

    def each(shape, kind):
        return [pltpu.VMEM(shape + (w,), kind) for w in WIDTHS]

    def hops():
        return [
            [[pltpu.VMEM((2 * rows if j > 0 and mode(ch, j, p) == "apart" else rows, w), BF16) for j in range(first + 1)]
             for ch, first in enumerate(FIRST)]
            for p, w in enumerate(WIDTHS)
        ]

    def crossings():
        return [pltpu.VMEM((1 + len(joints(p)), rows, w), BF16) for p, w in enumerate(WIDTHS)]

    most = max(FIRST) + 1
    nx = 1 + max(len(joints(p)) for p in range(PIECES))
    scratch = [
        pltpu.VMEM((6, tokens, kd), BF16), dma((6,)),
        each((2 * kd,), BF16), dma((PIECES,)), dma((PIECES,)), dma((PIECES,)), each((kd,), BF16), dma((PIECES,)),
        pltpu.VMEM((2 * tokens, 2 * kd), BF16), dma((2,)), dma((2,)),
        pltpu.VMEM((rows, half), BF16), dma, dma, dma,
        pltpu.VMEM((BLK, BLK), BF16), pltpu.VMEM((1, width), F32), pltpu.VMEM((1, width), F32), dma, dma,
        pltpu.VMEM((1, width), jnp.int32),
        each((2 * tokens,), F32),
        hops(), hops(), dma((2, most, PIECES)),
        crossings(), crossings(), dma((nx, PIECES)),
        each((2, 2, mine), BF16), dma((2, 2, PIECES)), dma((PIECES,)),
        each((rows,), F32), each((mine,), F32), each((mine,), BF16), each((mine,), BF16),
        dma((PIECES,)),
    ]
    operands = (
        leave_query, leave_key, leave_value, arrive_query, arrive_key, arrive_value,
        leave_residual, out_weight, gate_scale, sign_bits.reshape(1, width),
    )
    return pl.pallas_call(
        kernel,
        out_shape=pltpu.VMEM((1, mine, width), BF16),
        in_specs=[pl.BlockSpec(memory_space=pltpu.HBM)] * len(operands),
        out_specs=pl.BlockSpec(memory_space=pltpu.VMEM),
        scratch_shapes=scratch,
        compiler_params=pltpu.CompilerParams(
            collective_id=0, has_side_effects=True, vmem_limit_bytes=48 * 1024 * 1024),
        cost_estimate=pl.CostEstimate(
            flops=2 * 2 * tokens * kd * width, bytes_accessed=2 * kd * width, transcendentals=0),
    )(*(pltpu.with_memory_space_constraint(x, pltpu.HBM) for x in operands))


def solution(mesh):
    placed = (
        P("section", None, "tp"),
        P("section", None, "tp"),
        P("section", None, "tp"),
        P("section", None, "tp"),
        P("section", None, "tp"),
        P("section", None, "tp"),
        P("section", "tp", None),
        P("section", "tp", None),
        P("section", None),
        P(),
    )
    return jax.shard_map(
        local, mesh=mesh, in_specs=placed, out_specs=P("section", "tp", None), check_vma=False
    )
```

```python
import math

import jax
import jax.numpy as jnp
from jax import lax
from jax.experimental import pallas as pl
from jax.experimental.pallas import tpu as pltpu
from jax.sharding import PartitionSpec as P

HD = 128
BLK = 128
MESH = pl.DeviceIdType.MESH
F32 = jnp.float32
BF16 = jnp.bfloat16
WIDTHS = (768, 1280, 1024)
FIRST = (4, 3)
MODES = (
    (("next", "next", "apart", "apart"), ("next", "back", "back")),
    (("next", "next", "apart", "apart"), ("next", "back", "back")),
    (("next", "next", "apart", "apart"), ("next", "back", "back")),
)
ORDER = (
    ("P", 0), ("cB3", 0), ("A4", 0), ("cA1", 0), ("P", 1), ("A4", 1), ("cO", 0), ("P", 2), ("cB3", 1), ("A4", 2),
    ("cA1", 2), ("cO", 1), ("cB2", 0), ("jB3", 0), ("cB3", 2), ("A3", 0), ("cA1", 1), ("cB2", 1), ("A3", 1),
    ("jB3", 1), ("cO", 2), ("cB2", 2), ("A3", 2), ("jB3", 2), ("cA2", 0), ("jO", 0), ("jB2", 0), ("jO", 1),
    ("cA2", 1), ("jB2", 1), ("cA2", 2), ("jB2", 2), ("cB1", 0), ("cB1", 1), ("jA2", 0), ("jA2", 1), ("jA2", 2),
    ("jO", 2), ("cB1", 2), ("jB1", 0), ("jA1", 0), ("jA1", 1), ("jB1", 1), ("jA1", 2), ("jB1", 2), ("F", 0),
    ("F", 1), ("F", 2),
)
PIECES = len(WIDTHS)
STARTS = tuple(sum(WIDTHS[:p]) for p in range(PIECES))


def mode(ch, j, p):
    return MODES[p][ch][j - 1]


def joints(p):
    return [(ch, j) for ch, first in enumerate(FIRST) for j in range(1, first + 1) if mode(ch, j, p) != "apart"]


def kernel(
    lq, lk, lv, aq, ak, av, residual, weight, gate, sign_bits,
    out,
    qkv, qkv_sem,
    wbuf, w_sem, w_send, w_recv, wahead, ahead_sem,
    att, att_send, att_recv,
    resbuf, res_sem, res_send, res_recv,
    table, signs, gates, gate_sem, sign_sem, bits_v,
    sums,
    zs, zr, zr_sem,
    xs, xr, xr_sem,
    fin, fin_sem, sent,
    own0, own_keep, own_s, own_r, or_sem,
):
    sections = lax.axis_size("section")
    chips = lax.axis_size("tp") // 2
    s = lax.axis_index("section")
    tp = lax.axis_index("tp")
    z = tp >> 1
    c = tp & 1
    other = 1 - c
    tokens = lq.shape[1]
    kd = lq.shape[2]
    width = residual.shape[2]
    half = width // 2
    rows = tokens // chips
    mine = rows // 2

    def wrapped(at, count):
        return jnp.where(at < 0, at + count, jnp.where(at >= count, at - count, at))

    side = 1 - 2 * c
    around = {k: wrapped(z + k * side, chips) for k in range(-max(FIRST), max(FIRST) + 1)}
    row_of = {k: pl.multiple_of(rows * at, rows) for k, at in around.items()}
    near = {k: {"section": s, "tp": 2 * around[k] + c} for k in (-1, 1)}
    near_core = {(k, core): {"section": s, "tp": 2 * around[k] + core} for k in (-1, 1) for core in (0, 1)}
    next_section = {"section": wrapped(s + 1, sections), "tp": tp}
    prev_section = {"section": wrapped(s - 1, sections), "tp": tp}
    partner = {"section": s, "tp": 2 * z + other}

    barrier = pltpu.get_barrier_semaphore()
    greeted = [partner, next_section, prev_section] + list(near_core.values())
    for device in greeted:
        pl.semaphore_signal(barrier, inc=1, device_id=device, device_id_type=MESH)

    def toward(ch, p):
        return 1 if (ch + p) % 2 == 0 else -1

    def cols(p, which):
        return pl.ds(pl.multiple_of(which * half + STARTS[p], 128), WIDTHS[p])

    loads = []
    for i, ref in enumerate((lq, lk, lv, aq, ak, av)):
        loads.append(pltpu.make_async_copy(ref.at[0], qkv.at[i], qkv_sem.at[i]))
        loads[-1].start()

    def w_local(p):
        return pltpu.make_async_copy(weight.at[0, :, cols(p, c)], wbuf[p].at[pl.ds(0, kd)], w_sem.at[p])

    def w_ahead(p):
        return pltpu.make_async_copy(weight.at[0, :, cols(p, other)], wahead[p], ahead_sem.at[p])

    def send_weights(p):
        w_ahead(p).wait()
        w_remote(p).start()

    def w_remote(p):
        return pltpu.make_async_remote_copy(
            wahead[p], wbuf[p].at[pl.ds(kd, kd)], w_send.at[p], w_recv.at[p],
            device_id=partner, device_id_type=MESH)

    for p in range(PIECES):
        w_ahead(p).start()
    for p in range(PIECES):
        w_local(p).start()
    gate_copy = pltpu.make_async_copy(gate, gates, gate_sem)
    gate_copy.start()
    sign_copy = pltpu.make_async_copy(sign_bits, bits_v, sign_sem)
    sign_copy.start()
    own_rows = pl.ds(pl.multiple_of(mine * c, mine), mine)
    other_rows = pl.ds(pl.multiple_of(mine * other, mine), mine)
    res_local = pltpu.make_async_copy(
        residual.at[0, :, pl.ds(pl.multiple_of(c * half, 128), half)], resbuf.at[own_rows], res_sem)
    res_local.start()

    pl.semaphore_wait(barrier, len(greeted))

    res_remote = pltpu.make_async_remote_copy(
        residual.at[0, :, pl.ds(pl.multiple_of(other * half, 128), half)], resbuf.at[own_rows], res_send, res_recv,
        device_id=partner, device_id_type=MESH)
    res_remote.start()
    send_weights(0)

    def att_copy(m):
        there = att.at[pl.ds(m * tokens, tokens), pl.ds(kd, kd)]
        here = att.at[pl.ds(m * tokens, tokens), pl.ds(0, kd)]
        return pltpu.make_async_remote_copy(
            here, there, att_send.at[m], att_recv.at[m], device_id=partner, device_id_type=MESH)

    for m in range(2):
        for i in range(3):
            loads[3 * m + i].wait()
        for h in range(kd // HD):
            lanes = pl.ds(h * HD, HD)
            query, key, value = (qkv[3 * m + i, :, lanes] for i in range(3))
            scores = lax.dot_general(query, key, (((1,), (1,)), ((), ())), preferred_element_type=F32)
            scores = scores * (1.0 / math.sqrt(HD))
            peak = jnp.max(scores, axis=-1, keepdims=True)
            raised = jnp.exp(scores - peak)
            probs = (raised / jnp.sum(raised, axis=-1, keepdims=True)).astype(BF16)
            mixed = jnp.dot(probs, value, preferred_element_type=F32)
            att[pl.ds(m * tokens, tokens), lanes] = mixed.astype(BF16)
        att_copy(m).start()
    for p in range(1, PIECES):
        send_weights(p)

    i = lax.broadcasted_iota(jnp.int32, (BLK, BLK), 0)
    j = lax.broadcasted_iota(jnp.int32, (BLK, BLK), 1)
    anded = i & j
    anded = anded ^ (anded >> 4)
    anded = anded ^ (anded >> 2)
    anded = anded ^ (anded >> 1)
    table[...] = (1 - 2 * (anded & 1)).astype(F32).astype(BF16)
    sign_copy.wait()
    signs[...] = 1.0 - 2.0 * bits_v[...].astype(F32)

    def turned(values):
        r, n = values.shape[0], values.shape[1] // BLK
        blocks = jnp.concatenate([values[:, b * BLK:(b + 1) * BLK] for b in range(n)], axis=0)
        made = jnp.dot(blocks, table[...], preferred_element_type=F32)
        return jnp.concatenate([made[b * r:(b + 1) * r] for b in range(n)], axis=1)

    gate_copy.wait()

    def leaving(p, at):
        return sums[p][pl.ds(row_of[at], rows), :]

    def arriving(p, at):
        return sums[p][pl.ds(pl.multiple_of(tokens + row_of[at], rows), rows), :]

    def z_copy(ch, j, p):
        to = near[toward(ch, p)]
        return pltpu.make_async_remote_copy(
            zs[p][ch][j], zr[p][ch][j], sent.at[p], zr_sem.at[ch, j, p], device_id=to, device_id_type=MESH)

    def fin_copy(ch, core, p):
        to = near_core[toward(ch, p), core]
        return pltpu.make_async_remote_copy(
            zs[p][ch][1].at[pl.ds(core * mine, mine)], fin[p].at[ch, c],
            sent.at[p], fin_sem.at[p], device_id=to, device_id_type=MESH)

    def fin_arrivals(p):
        whole = wbuf[p].at[pl.ds(0, 4 * mine)]
        return pltpu.make_async_copy(whole, whole, fin_sem.at[p])

    def x_copy(at, p):
        to = next_section if at == 0 or mode(*joints(p)[at - 1], p) == "next" else prev_section
        return pltpu.make_async_remote_copy(
            xs[p].at[at], xr[p].at[at], sent.at[p], xr_sem.at[at, p], device_id=to, device_id_type=MESH)

    def slot(ch, j, p):
        return joints(p).index((ch, j)) + 1

    def own_copy(p):
        return pltpu.make_async_remote_copy(
            own_s[p], own_r[p], sent.at[p], or_sem.at[p], device_id=partner, device_id_type=MESH)

    def target(ch, j, p):
        return j * toward(ch, p)

    def come(ch, j, p, arrived):
        kind = mode(ch, j + 1, p) if j < FIRST[ch] else None
        if kind == "apart":
            return zr[p][ch][j + 1][rows:] if arrived else zr[p][ch][j + 1][:rows]
        if kind == ("next" if arrived else "back"):
            return zr[p][ch][j + 1][...]
        return None

    def plus(sums_here, other_sums):
        return sums_here if other_sums is None else sums_here + other_sums.astype(F32)

    def apart(ch, j, p):
        if j < FIRST[ch]:
            z_copy(ch, j + 1, p).wait_recv()
        at = target(ch, j, p)
        zs[p][ch][j][:rows] = plus(leaving(p, at), come(ch, j, p, False)).astype(BF16)
        zs[p][ch][j][rows:] = plus(arriving(p, at), come(ch, j, p, True)).astype(BF16)
        z_copy(ch, j, p).start()

    def cross(ch, j, p):
        arrived = mode(ch, j, p) == "back"
        own = (arriving if arrived else leaving)(p, target(ch, j, p))
        if come(ch, j, p, arrived) is not None:
            z_copy(ch, j + 1, p).wait_recv()
        xs[p][slot(ch, j, p)] = plus(own, come(ch, j, p, arrived)).astype(BF16)
        x_copy(slot(ch, j, p), p).start()

    def joined(ch, j, p):
        arrived = mode(ch, j, p) == "next"
        own = (arriving if arrived else leaving)(p, target(ch, j, p))
        x_copy(slot(ch, j, p), p).wait_recv()
        own = own + xr[p][slot(ch, j, p)].astype(F32)
        if come(ch, j, p, arrived) is not None and come(ch, j, p, not arrived) is None:
            z_copy(ch, j + 1, p).wait_recv()
        zs[p][ch][j][...] = plus(own, come(ch, j, p, arrived)).astype(BF16)
        if j > 1:
            z_copy(ch, j, p).start()
        else:
            for core in (0, 1):
                fin_copy(ch, core, p).start()

    def own_cross(p):
        if p == ORDER[[step for step, _ in ORDER].index("cO")][1]:
            res_local.wait()
            res_remote.wait_recv()
        plain = turned(resbuf[:, pl.ds(STARTS[p], WIDTHS[p])])
        plain = plain * (signs[:, cols(p, c)] * (1.0 / math.sqrt(BLK)))
        xs[p][0] = (leaving(p, 0) + plain).astype(BF16)
        x_copy(0, p).start()

    def own_joined(p):
        x_copy(0, p).wait_recv()
        own0[p][...] = arriving(p, 0) + xr[p][0].astype(F32)
        own_keep[p][...] = own0[p][own_rows, :]
        own_s[p][...] = own0[p][other_rows, :].astype(BF16)
        own_copy(p).start()

    def project(p):
        if p > 0:
            w_local(p).wait()
            w_remote(p).wait_recv()
            made = jnp.dot(att[...], wbuf[p][...], preferred_element_type=F32)
            sums[p][...] = made * gates[:, cols(p, c)]
            return
        w_local(p).wait()
        sums[p][...] = jnp.dot(att[:, :kd], wbuf[p][:kd], preferred_element_type=F32)
        for m in range(2):
            att_copy(m).wait_recv()
        w_remote(p).wait_recv()
        made = sums[p][...] + jnp.dot(att[:, kd:], wbuf[p][kd:], preferred_element_type=F32)
        sums[p][...] = made * gates[:, cols(p, c)]

    def finish(p):
        own_copy(p).wait_recv()
        fin_arrivals(p).wait()
        for core, own in ((c, own_keep[p][...]), (other, own_r[p][...].astype(F32))):
            total = own + fin[p][0, core].astype(F32) + fin[p][1, core].astype(F32)
            total = total * signs[:, cols(p, core)]
            high = total.astype(BF16)
            low = (total - high.astype(F32)).astype(BF16)
            r = turned(jnp.concatenate([high, low], axis=0))
            r = (r[:mine] + r[mine:]) * (1.0 / math.sqrt(BLK))
            out[0, :, cols(p, core)] = r.astype(BF16)

    for step, p in ORDER:
        if step == "P":
            project(p)
        elif step == "F":
            finish(p)
        elif step == "cO":
            own_cross(p)
        elif step == "jO":
            own_joined(p)
        else:
            ch, j = "AB".index(step[-2]), int(step[-1])
            (cross if step[0] == "c" else joined if step[0] == "j" else apart)(ch, j, p)

    res_remote.wait_send()
    for m in range(2):
        att_copy(m).wait_send()
    for p in range(PIECES):
        w_remote(p).wait_send()
        count = mine + rows * (1 + len(joints(p)) + len(FIRST))
        for ch, first in enumerate(FIRST):
            count += sum(zs[p][ch][j].shape[0] for j in range(2, first + 1))
        whole = wbuf[p].at[pl.ds(0, count)]
        pltpu.make_async_copy(whole, whole, sent.at[p]).wait()


def local(
    leave_query, leave_key, leave_value, arrive_query, arrive_key, arrive_value,
    leave_residual, out_weight, gate_scale, sign_bits,
):
    tokens, kd = leave_query.shape[1:]
    width = leave_residual.shape[2]
    chips = lax.axis_size("tp") // 2
    rows, mine = tokens // chips, tokens // chips // 2
    half = width // 2
    dma = pltpu.SemaphoreType.DMA

    def each(shape, kind):
        return [pltpu.VMEM(shape + (w,), kind) for w in WIDTHS]

    def hops():
        return [
            [[pltpu.VMEM((2 * rows if j > 0 and mode(ch, j, p) == "apart" else rows, w), BF16) for j in range(first + 1)]
             for ch, first in enumerate(FIRST)]
            for p, w in enumerate(WIDTHS)
        ]

    def crossings():
        return [pltpu.VMEM((1 + len(joints(p)), rows, w), BF16) for p, w in enumerate(WIDTHS)]

    most = max(FIRST) + 1
    nx = 1 + max(len(joints(p)) for p in range(PIECES))
    scratch = [
        pltpu.VMEM((6, tokens, kd), BF16), dma((6,)),
        each((2 * kd,), BF16), dma((PIECES,)), dma((PIECES,)), dma((PIECES,)), each((kd,), BF16), dma((PIECES,)),
        pltpu.VMEM((2 * tokens, 2 * kd), BF16), dma((2,)), dma((2,)),
        pltpu.VMEM((rows, half), BF16), dma, dma, dma,
        pltpu.VMEM((BLK, BLK), BF16), pltpu.VMEM((1, width), F32), pltpu.VMEM((1, width), F32), dma, dma,
        pltpu.VMEM((1, width), jnp.int32),
        each((2 * tokens,), F32),
        hops(), hops(), dma((2, most, PIECES)),
        crossings(), crossings(), dma((nx, PIECES)),
        each((2, 2, mine), BF16), dma((PIECES,)), dma((PIECES,)),
        each((rows,), F32), each((mine,), F32), each((mine,), BF16), each((mine,), BF16),
        dma((PIECES,)),
    ]
    operands = (
        leave_query, leave_key, leave_value, arrive_query, arrive_key, arrive_value,
        leave_residual, out_weight, gate_scale, sign_bits.reshape(1, width),
    )
    return pl.pallas_call(
        kernel,
        out_shape=pltpu.VMEM((1, mine, width), BF16),
        in_specs=[pl.BlockSpec(memory_space=pltpu.HBM)] * len(operands),
        out_specs=pl.BlockSpec(memory_space=pltpu.VMEM),
        scratch_shapes=scratch,
        compiler_params=pltpu.CompilerParams(
            collective_id=0, has_side_effects=True, vmem_limit_bytes=48 * 1024 * 1024),
        cost_estimate=pl.CostEstimate(
            flops=2 * 2 * tokens * kd * width, bytes_accessed=2 * kd * width, transcendentals=0),
    )(*(pltpu.with_memory_space_constraint(x, pltpu.HBM) for x in operands))


def solution(mesh):
    placed = (
        P("section", None, "tp"),
        P("section", None, "tp"),
        P("section", None, "tp"),
        P("section", None, "tp"),
        P("section", None, "tp"),
        P("section", None, "tp"),
        P("section", "tp", None),
        P("section", "tp", None),
        P("section", None),
        P(),
    )
    return jax.shard_map(
        local, mesh=mesh, in_specs=placed, out_specs=P("section", "tp", None), check_vma=False
    )
```
